32 devices in a mesh: dp: 8 (over z, x), seq: 4 (over y, core).
Axes of the slice: x: 2, y: 2, z: 4, core: 2. Of those that a mesh axis runs over, the one named last changes fastest.
Arguments:
- hidden: bfloat16 [8, 3072, 2560], P('dp', 'seq'), may hold values from -6 to 6
- log_decay: float32 [8, 40, 3072], P('dp', None, 'seq'), may hold values from -2 to 0, as said below
- input_weight: bfloat16 [2816, 2560], P(('dp', 'seq')), may hold values from -0.125 to 0.125
- conv_weight: bfloat16 [4, 2816], replicated, may hold values from -3 to 3
- conv_bias: float32 [2816], replicated, may hold values from -0.5 to 0.5
- skip_gain: float32 [40], replicated, may hold values from 0.5 to 1.5
Outputs:
- mixer_out: bfloat16 [8, 3072, 2560], P('dp', 'seq')
The draws below stay inside these ranges and needn't reach their ends.
Inputs may be any that keep to these rules, and one draw needn't show every extreme that they name: `log_decay`: every value is negative.
All inputs are finite; a program needn't handle non-finite values.
Results may differ from the reference program's by a relative error of at most 0.0064.
Values may be sent and summed in bfloat16 or wider, within the bound.
A program may use at most 128 MiB of HBM per device.

```python
import math
import jax
import jax.numpy as jnp
from jax import lax

D = 2560
HALF_HEADS = 40
HEAD_DIM = 64
STATE = 128
SPAN = 256
CONV = 4
TOK_DEV = 768
INNER = 2560
COLS = 2816
BATCH_CONTEXTS = 8
CONTEXT_LENGTH = 3072


def draw_log_decay(key, part):
    random_keys = jax.random.split(key, 7)
    fast_share = 0.5
    blocks = CONTEXT_LENGTH // TOK_DEV
    fast = (jax.random.uniform(random_keys[0], (BATCH_CONTEXTS, HALF_HEADS, 1)) < fast_share).astype(jnp.float32)
    slow_rate = jax.random.uniform(random_keys[1], (BATCH_CONTEXTS, HALF_HEADS, 1), minval=0.3, maxval=0.9) / CONTEXT_LENGTH
    fast_rate = jax.random.uniform(random_keys[2], (BATCH_CONTEXTS, HALF_HEADS, 1), minval=5.0, maxval=8.0) / SPAN
    baseline_rate = fast * fast_rate + (1.0 - fast) * slow_rate
    shard_multiplier = jnp.exp(jax.random.uniform(random_keys[3], (BATCH_CONTEXTS, HALF_HEADS, blocks, 1), minval=math.log(0.5), maxval=math.log(1.5)))
    shard_multiplier = jnp.broadcast_to(shard_multiplier, (BATCH_CONTEXTS, HALF_HEADS, blocks, TOK_DEV)).reshape(BATCH_CONTEXTS, HALF_HEADS, CONTEXT_LENGTH)
    jitter_level = jax.random.uniform(random_keys[4], (BATCH_CONTEXTS, HALF_HEADS, CONTEXT_LENGTH), minval=0.6, maxval=1.4)
    spike_position = jax.random.randint(random_keys[5], (BATCH_CONTEXTS, 4, 1), 0, CONTEXT_LENGTH)
    spike_strength = jnp.any(jnp.arange(CONTEXT_LENGTH)[None, None, :] == spike_position, axis=1, keepdims=True).astype(jnp.float32)
    spike_falloff = jax.random.uniform(random_keys[6], (BATCH_CONTEXTS, HALF_HEADS, 1), minval=0.22, maxval=0.69)
    return -(baseline_rate * shard_multiplier * jitter_level + spike_strength * spike_falloff)


def block_scale(own_key, extent, cuts, smallest, largest):
    def one(axis_at, parts):
        draws = jax.random.uniform(jax.random.fold_in(jax.random.fold_in(own_key, 6), axis_at), (parts,), jnp.float32, smallest / len(cuts), largest / len(cuts))
        return jnp.repeat(jnp.exp(draws), extent[axis_at] // parts).reshape((-1,) + (1,) * (len(extent) - axis_at - 1))

    level = one(*cuts[0])
    for cut in cuts[1:]:
        level = level * one(*cut)
    return level


def centred(key, dims, width, reach, cuts=(), dtype=jnp.bfloat16):
    loudness = block_scale(key, dims, cuts, -0.22, 0.18) if cuts else 1.0
    drawn = jax.random.normal(key, dims, jnp.float32) * width * loudness
    return jnp.minimum(jnp.maximum(drawn, -reach), reach).astype(dtype)


def setup_inputs(seed: int = 0) -> dict:
    arg_keys = jax.random.split(jax.random.key(seed), 7)
    hidden = centred(arg_keys[0], (BATCH_CONTEXTS, CONTEXT_LENGTH, D), 1.0, 6.0, ((0, 8), (1, 4)))
    log_decay = draw_log_decay(jax.random.fold_in(arg_keys[6], 71), 0)
    input_weight = centred(arg_keys[2], (COLS, D), D ** -0.5, 0.125, ((0, 32),))
    conv_weight = centred(arg_keys[3], (CONV, COLS), CONV ** -0.5, 3.0)
    conv_bias = jnp.clip(jax.random.uniform(arg_keys[4], (COLS,), jnp.float32, -0.5, 0.5), -0.5, 0.5)
    skip_gain = jnp.clip(jax.random.uniform(arg_keys[5], (HALF_HEADS,), jnp.float32, 0.5, 1.5), 0.5, 1.5)
    return dict(hidden=hidden, log_decay=log_decay, input_weight=input_weight, conv_weight=conv_weight, conv_bias=conv_bias, skip_gain=skip_gain)


def mixing_output(x_heads, b_span, c_span, cumulative, step_size):
    scores = jnp.dot(c_span, b_span.T, preferred_element_type=jnp.float32)
    span_len = cumulative.shape[1]
    causal = jnp.arange(span_len)[:, None] >= jnp.arange(span_len)[None, :]
    spread = jnp.where(causal[None], cumulative[:, :, None] - cumulative[:, None, :], -jnp.inf)
    mixing = (scores[None] * jnp.exp(spread) * step_size[:, None, :]).astype(jnp.bfloat16)
    return jnp.einsum("hqk,khp->qhp", mixing.astype(jnp.float32), x_heads.astype(jnp.float32))


def span_state(x_heads, b_span, cumulative, step_size):
    weight = jnp.exp(cumulative[:, -1:] - cumulative) * step_size
    decayed = (x_heads * weight.T[:, :, None]).astype(jnp.bfloat16)
    return jnp.einsum("khp,kn->hpn", decayed.astype(jnp.float32), b_span.astype(jnp.float32))


def state_output(c_span, entering, cumulative):
    readout = jnp.einsum("qn,hpn->qhp", c_span.astype(jnp.float32), entering, precision=lax.Precision.HIGHEST)
    return jnp.exp(cumulative).T[:, :, None] * readout


def reference(hidden, log_decay, input_weight, conv_weight, conv_bias, skip_gain):
    def one_context(operands):
        token_rows, decay_rows = operands
        projected = lax.dot_general(token_rows, input_weight, (((1,), (1,)), ((), ())), preferred_element_type=jnp.float32).astype(jnp.bfloat16)
        padded = jnp.concatenate([jnp.zeros((CONV - 1, COLS), jnp.bfloat16), projected], axis=0)
        filtered = jnp.broadcast_to(conv_bias[None, :], (CONTEXT_LENGTH, COLS))
        for kernel_tap in range(CONV):
            filtered = filtered + padded[kernel_tap:kernel_tap + CONTEXT_LENGTH].astype(jnp.float32) * conv_weight[kernel_tap].astype(jnp.float32)[None, :]
        active = jax.nn.silu(filtered).astype(jnp.bfloat16)
        span_count = CONTEXT_LENGTH // SPAN
        x_all = active[:, :INNER].reshape(span_count, SPAN, HALF_HEADS, HEAD_DIM)
        b_all = active[:, INNER:INNER + STATE].reshape(span_count, SPAN, STATE)
        c_all = active[:, INNER + STATE:].reshape(span_count, SPAN, STATE)
        decay_spans = decay_rows.reshape(HALF_HEADS, span_count, SPAN).transpose(1, 0, 2)
        cumulative = jnp.cumsum(decay_spans, axis=2)

        def advance(entering, inputs):
            x_heads, b_span, c_span, cum_span, decay_span = inputs
            step_size = -decay_span
            outputs = mixing_output(x_heads, b_span, c_span, cum_span, step_size) + state_output(c_span, entering, cum_span)
            new_state = jnp.exp(cum_span[:, -1])[:, None, None] * entering + span_state(x_heads, b_span, cum_span, step_size)
            return new_state, outputs

        start_state = jnp.zeros((HALF_HEADS, HEAD_DIM, STATE), jnp.float32)
        _, outputs = lax.scan(advance, start_state, (x_all, b_all, c_all, cumulative, decay_spans))
        outputs = outputs.reshape(CONTEXT_LENGTH, HALF_HEADS, HEAD_DIM) + skip_gain[None, :, None] * x_all.reshape(CONTEXT_LENGTH, HALF_HEADS, HEAD_DIM).astype(jnp.float32)
        return outputs.reshape(CONTEXT_LENGTH, INNER).astype(jnp.bfloat16)

    return lax.map(one_context, (hidden, log_decay))
```

```python
import functools

import jax
import jax.numpy as jnp
from jax import lax
from jax.experimental import pallas as pl
from jax.experimental.pallas import tpu as pltpu
from jax.sharding import PartitionSpec as P

HEADS = 40
HEAD_DIM = 64
STATE = 128
SPAN = 256
CONV = 4
INNER = 2560
COLS = 2816
GROUP = 8
GROUPS = HEADS // GROUP
CHUNK = 256
HALO = 16
TILE = 64
LOG2E = 1.4426950408889634
F32 = jnp.float32
BF16 = jnp.bfloat16
NT = (((1,), (1,)), ((), ()))


def split_parts(both):
    high = both.astype(BF16).astype(F32)
    lane = lax.broadcasted_iota(jnp.int32, both.shape, 1)
    return jnp.where(lane < HEADS, high, both - high).astype(BF16)


def mixer_kernel(
    spans, peers,
    proj, taps, bias, weight, growth, spread, decay, skip, column, row,
    out,
    halo, previous, act, bt, states, local, total, scores, sending, entering,
    halo_sems, state_sems,
):
    place = lax.axis_index("seq")
    length = spans * SPAN
    after, before = lax.rem(place + 1, peers), lax.rem(place + peers - 1, peers)
    barrier = pltpu.get_barrier_semaphore()
    for neighbour in (before, after):
        pl.semaphore_signal(
            barrier, inc=1, device_id={"seq": neighbour}, device_id_type=pl.DeviceIdType.MESH
        )
    pl.semaphore_wait(barrier, 2)
    has_after = place < peers - 1
    has_before = place > 0

    halo_copy = pltpu.make_async_remote_copy(
        src_ref=proj.at[pl.ds(length - HALO, HALO)], dst_ref=halo,
        send_sem=halo_sems.at[0], recv_sem=halo_sems.at[1],
        device_id={"seq": after}, device_id_type=pl.DeviceIdType.MESH,
    )
    state_copy = pltpu.make_async_remote_copy(
        src_ref=sending, dst_ref=entering,
        send_sem=state_sems.at[0], recv_sem=state_sems.at[1],
        device_id={"seq": after}, device_id_type=pl.DeviceIdType.MESH,
    )

    @pl.when(has_after)
    def _():
        halo_copy.start()

    def rows_of(span):
        return pl.ds(pl.multiple_of(span * SPAN, SPAN), SPAN)

    def lanes_of(chunk, width=CHUNK):
        return pl.ds(pl.multiple_of(chunk * width, width), width)

    @pl.loop(0, spans)
    def _(lap):
        span = spans - 1 - lap
        rows = rows_of(span)

        @pl.when(span > 0)
        def _():
            start = pl.multiple_of(jnp.maximum(span * SPAN - HALO, 0), HALO)
            previous[...] = proj[pl.ds(start, HALO), :]

        @pl.when(span == 0)
        def _():
            @pl.when(has_before)
            def _():
                halo_copy.wait_recv()
                previous[...] = halo[...]

            @pl.when(jnp.logical_not(has_before))
            def _():
                previous[...] = jnp.zeros_like(previous)

        @pl.loop(0, COLS // CHUNK)
        def _(chunk):
            lanes = lanes_of(chunk)
            tap = [taps[k : k + 1, lanes] for k in range(CONV)]
            offset = bias[:, lanes]
            for part in range(SPAN // TILE):
                start = pl.multiple_of(span * SPAN + part * TILE, TILE)
                here = proj[pl.ds(start, TILE), lanes].astype(F32)
                if part == 0:
                    ahead = previous[:, lanes].astype(F32)
                else:
                    earlier = pl.multiple_of(start - HALO, HALO)
                    ahead = proj[pl.ds(earlier, HALO), lanes].astype(F32)
                both = jnp.concatenate([ahead[HALO - 8 :], here], axis=0)
                value = offset + here * tap[CONV - 1]
                for k in range(CONV - 1):
                    at = 8 - (CONV - 1) + k
                    value = value + both[at : at + TILE] * tap[k]
                act[pl.ds(start, TILE), lanes] = (value / (1.0 + jnp.exp(-value))).astype(BF16)

        bt[...] = act[rows, INNER : INNER + STATE].astype(F32).T.astype(BF16)
        parts = split_parts(weight[rows, :])

        @pl.loop(0, INNER // CHUNK)
        def _(chunk):
            lanes = lanes_of(chunk)
            scale = jnp.dot(parts, spread[:, lanes], preferred_element_type=F32)
            decayed = (act[rows, lanes].astype(F32) * scale).astype(BF16)
            states[span, :, lanes] = jnp.dot(bt[...], decayed, preferred_element_type=F32)

    @pl.loop(0, INNER // CHUNK)
    def _(chunk):
        lanes = lanes_of(chunk)
        held = states[0, :, lanes]
        for span in range(1, spans):
            held = decay[span : span + 1, lanes] * held + states[span, :, lanes]
        local[:, lanes] = held

    def relay():
        @pl.when(has_before)
        def _():
            state_copy.wait_recv()

        @pl.when(jnp.logical_not(has_before))
        def _():
            entering[...] = jnp.zeros_like(entering)

        @pl.when(has_after)
        def _():
            @pl.loop(0, INNER // CHUNK)
            def _(chunk):
                lanes = lanes_of(chunk)
                whole = decay[spans : spans + 1, lanes]
                sending[:, lanes] = (
                    whole * entering[:, lanes].astype(F32) + local[:, lanes]
                ).astype(BF16)

            state_copy.start()

    @pl.when(place <= 1)
    def _():
        relay()

    @pl.loop(0, spans)
    def _(span):
        rows = rows_of(span)
        product = lax.dot_general(
            act[rows, INNER + STATE :], act[rows, INNER : INNER + STATE], NT,
            preferred_element_type=F32,
        )
        later = lax.broadcasted_iota(jnp.int32, (SPAN, SPAN), 0)
        sooner = lax.broadcasted_iota(jnp.int32, (SPAN, SPAN), 1)
        scores[...] = jnp.where(later >= sooner, product, 0.0)
        half = SPAN // 2
        first = lax.broadcasted_iota(jnp.int32, (SPAN, 2 * HEAD_DIM), 1) < HEAD_DIM

        @pl.loop(0, GROUPS)
        def _(group):
            for pair in range(GROUP // 2):
                lanes = pl.ds(
                    pl.multiple_of(group * (GROUP * HEAD_DIM) + pair * 128, 128), 128
                )
                heads_in = act[rows, lanes]
                given = []
                for head in (2 * pair, 2 * pair + 1):
                    at_later = column[group, rows, head : head + 1]
                    at_sooner = row[group, head : head + 1, rows]
                    upper = scores[:half, :half] * jnp.exp2(
                        jnp.minimum(at_later[:half] - at_sooner[:, :half], 100.0)
                    )
                    lower = scores[half:, :] * jnp.exp2(
                        jnp.minimum(at_later[half:] - at_sooner, 100.0)
                    )
                    given.append(
                        jnp.concatenate(
                            [
                                jnp.dot(
                                    upper.astype(BF16), heads_in[:half],
                                    preferred_element_type=F32,
                                ),
                                jnp.dot(
                                    lower.astype(BF16), heads_in, preferred_element_type=F32
                                ),
                            ],
                            axis=0,
                        )
                    )
                total[rows, lanes] = (
                    jnp.where(first, given[0], given[1])
                    + skip[:, lanes] * heads_in.astype(F32)
                )

    @pl.when(place > 1)
    def _():
        relay()

    @pl.loop(0, INNER // CHUNK)
    def _(chunk):
        lanes = lanes_of(chunk)
        held = entering[:, lanes].astype(F32)
        for span in range(spans):
            rows = pl.ds(span * SPAN, SPAN)
            grown = jnp.dot(
                split_parts(growth[rows, :]), spread[:, lanes], preferred_element_type=F32
            )
            read = jnp.dot(
                act[rows, INNER + STATE :], held.astype(BF16), preferred_element_type=F32
            )
            out[rows, lanes] = (total[rows, lanes] + grown * read).astype(BF16)
            if span < spans - 1:
                held = decay[span : span + 1, lanes] * held + states[span, :, lanes]

    @pl.when(has_after)
    def _():
        halo_copy.wait_send()
        state_copy.wait_send()


def mixer(projected, log_decay, conv_weight, conv_bias, skip_gain):
    length = projected.shape[0]
    spans = length // SPAN
    peers = lax.axis_size("seq")
    step = -log_decay
    cum = jnp.cumsum(log_decay.reshape(HEADS, spans, SPAN), axis=2)
    last = cum[:, :, -1:]
    weight = jnp.exp(last - cum).reshape(HEADS, length) * step
    flat = cum.reshape(HEADS, length)

    def doubled(a):
        return jnp.pad(jnp.concatenate([a, a], axis=0).T, ((0, 0), (0, 128 - 2 * HEADS)))

    grouped = (flat * LOG2E).reshape(GROUPS, GROUP, length)
    column = grouped.transpose(0, 2, 1)
    row = grouped - jnp.log2(step).reshape(GROUPS, GROUP, length)
    totals = last[:, :, 0].T
    totals = jnp.concatenate([totals, jnp.sum(totals, axis=0, keepdims=True)], axis=0)
    decay = jnp.repeat(jnp.exp(totals), HEAD_DIM, axis=1)
    decay = jnp.pad(decay, ((0, -decay.shape[0] % 8), (0, 0)))
    head_of = jnp.arange(INNER)[None, :] // HEAD_DIM
    part = jnp.arange(128)[:, None]
    spread = ((part % HEADS == head_of) & (part < 2 * HEADS)).astype(BF16)
    taps = jnp.pad(conv_weight.astype(F32), ((0, 8 - CONV), (0, 0)))
    vmem = pl.BlockSpec(memory_space=pltpu.VMEM)
    return pl.pallas_call(
        functools.partial(mixer_kernel, spans, peers),
        out_shape=jax.ShapeDtypeStruct((length, INNER), BF16),
        in_specs=[vmem] * 10,
        out_specs=vmem,
        scratch_shapes=[
            pltpu.VMEM((HALO, COLS), BF16),
            pltpu.VMEM((HALO, COLS), BF16),
            pltpu.VMEM((length, COLS), BF16),
            pltpu.VMEM((STATE, SPAN), BF16),
            pltpu.VMEM((spans, STATE, INNER), F32),
            pltpu.VMEM((STATE, INNER), F32),
            pltpu.VMEM((length, INNER), F32),
            pltpu.VMEM((SPAN, SPAN), F32),
            pltpu.VMEM((STATE, INNER), BF16),
            pltpu.VMEM((STATE, INNER), BF16),
            pltpu.SemaphoreType.DMA((2,)),
            pltpu.SemaphoreType.DMA((2,)),
        ],
        compiler_params=pltpu.CompilerParams(
            collective_id=0, has_side_effects=True, vmem_limit_bytes=56 * 2**20
        ),
        cost_estimate=pl.CostEstimate(
            flops=8 * 10**9, bytes_accessed=16 * 10**6, transcendentals=12 * 10**6
        ),
        name="mixer",
    )(
        projected, taps, conv_bias[None, :], doubled(weight), doubled(jnp.exp(flat)),
        spread, decay, jnp.repeat(skip_gain, HEAD_DIM)[None, :], column, row,
    )


def body(hidden, log_decay, input_weight, conv_weight, conv_bias, skip_gain):
    projected = lax.dot_general(
        hidden[0],
        lax.all_gather(input_weight, ("dp", "seq"), axis=0, tiled=True),
        NT,
        preferred_element_type=F32,
    ).astype(BF16)
    return mixer(projected, log_decay[0], conv_weight, conv_bias, skip_gain)[None]


def solution(mesh):
    placed = (P("dp", "seq", None), P("dp", None, "seq"), P(("dp", "seq"), None), P(), P(), P())
    return jax.shard_map(
        body, mesh=mesh, in_specs=placed, out_specs=P("dp", "seq", None), check_vma=False
    )
```

```python
import functools

import jax
import jax.numpy as jnp
from jax import lax
from jax.experimental import pallas as pl
from jax.experimental.pallas import tpu as pltpu
from jax.sharding import PartitionSpec as P

HEADS = 40
HEAD_DIM = 64
STATE = 128
SPAN = 256
CONV = 4
INNER = 2560
COLS = 2816
GROUP = 8
GROUPS = HEADS // GROUP
CHUNK = 256
HALO = 16
TILE = 64
LOG2E = 1.4426950408889634
F32 = jnp.float32
BF16 = jnp.bfloat16
NT = (((1,), (1,)), ((), ()))


def split_parts(both):
    high = both.astype(BF16).astype(F32)
    lane = lax.broadcasted_iota(jnp.int32, both.shape, 1)
    return jnp.where(lane < HEADS, high, both - high).astype(BF16)


def mixer_kernel(
    spans, peers,
    proj, taps, bias, weight, growth, spread, decay, skip, column, row,
    out,
    halo, previous, act, bt, states, local, total, scores, sending, entering,
    halo_sems, state_sems,
):
    place = lax.axis_index("seq")
    length = spans * SPAN
    after, before = lax.rem(place + 1, peers), lax.rem(place + peers - 1, peers)
    barrier = pltpu.get_barrier_semaphore()
    for neighbour in (before, after):
        pl.semaphore_signal(
            barrier, inc=1, device_id={"seq": neighbour}, device_id_type=pl.DeviceIdType.MESH
        )
    pl.semaphore_wait(barrier, 2)
    has_after = place < peers - 1
    has_before = place > 0

    halo_copy = pltpu.make_async_remote_copy(
        src_ref=proj.at[pl.ds(length - HALO, HALO)], dst_ref=halo,
        send_sem=halo_sems.at[0], recv_sem=halo_sems.at[1],
        device_id={"seq": after}, device_id_type=pl.DeviceIdType.MESH,
    )
    state_copy = pltpu.make_async_remote_copy(
        src_ref=sending, dst_ref=entering,
        send_sem=state_sems.at[0], recv_sem=state_sems.at[1],
        device_id={"seq": after}, device_id_type=pl.DeviceIdType.MESH,
    )

    @pl.when(has_after)
    def _():
        halo_copy.start()

    def rows_of(span):
        return pl.ds(pl.multiple_of(span * SPAN, SPAN), SPAN)

    def lanes_of(chunk, width=CHUNK):
        return pl.ds(pl.multiple_of(chunk * width, width), width)

    @pl.loop(0, spans)
    def _(lap):
        span = spans - 1 - lap
        rows = rows_of(span)

        @pl.when(span > 0)
        def _():
            start = pl.multiple_of(jnp.maximum(span * SPAN - HALO, 0), HALO)
            previous[...] = proj[pl.ds(start, HALO), :]

        @pl.when(span == 0)
        def _():
            @pl.when(has_before)
            def _():
                halo_copy.wait_recv()
                previous[...] = halo[...]

            @pl.when(jnp.logical_not(has_before))
            def _():
                previous[...] = jnp.zeros_like(previous)

        @pl.loop(0, COLS // CHUNK)
        def _(chunk):
            lanes = lanes_of(chunk)
            tap = [taps[k : k + 1, lanes] for k in range(CONV)]
            offset = bias[:, lanes]
            for part in range(SPAN // TILE):
                start = pl.multiple_of(span * SPAN + part * TILE, TILE)
                here = proj[pl.ds(start, TILE), lanes].astype(F32)
                if part == 0:
                    ahead = previous[:, lanes].astype(F32)
                else:
                    earlier = pl.multiple_of(start - HALO, HALO)
                    ahead = proj[pl.ds(earlier, HALO), lanes].astype(F32)
                both = jnp.concatenate([ahead[HALO - 8 :], here], axis=0)
                value = offset + here * tap[CONV - 1]
                for k in range(CONV - 1):
                    at = 8 - (CONV - 1) + k
                    value = value + both[at : at + TILE] * tap[k]
                act[pl.ds(start, TILE), lanes] = (value / (1.0 + jnp.exp(-value))).astype(BF16)

        bt[...] = act[rows, INNER : INNER + STATE].astype(F32).T.astype(BF16)
        parts = split_parts(weight[rows, :])

        @pl.loop(0, INNER // CHUNK)
        def _(chunk):
            lanes = lanes_of(chunk)
            scale = jnp.dot(parts, spread[:, lanes], preferred_element_type=F32)
            decayed = (act[rows, lanes].astype(F32) * scale).astype(BF16)
            states[span, :, lanes] = jnp.dot(bt[...], decayed, preferred_element_type=F32)

    @pl.loop(0, INNER // CHUNK)
    def _(chunk):
        lanes = lanes_of(chunk)
        held = states[0, :, lanes]
        for span in range(1, spans):
            held = decay[span : span + 1, lanes] * held + states[span, :, lanes]
        local[:, lanes] = held

    def relay():
        @pl.when(has_before)
        def _():
            state_copy.wait_recv()

        @pl.when(jnp.logical_not(has_before))
        def _():
            entering[...] = jnp.zeros_like(entering)

        @pl.when(has_after)
        def _():
            @pl.loop(0, INNER // CHUNK)
            def _(chunk):
                lanes = lanes_of(chunk)
                whole = decay[spans : spans + 1, lanes]
                sending[:, lanes] = (
                    whole * entering[:, lanes].astype(F32) + local[:, lanes]
                ).astype(BF16)

            state_copy.start()

    @pl.when(place <= 1)
    def _():
        relay()

    @pl.loop(0, spans)
    def _(span):
        rows = rows_of(span)
        product = lax.dot_general(
            act[rows, INNER + STATE :], act[rows, INNER : INNER + STATE], NT,
            preferred_element_type=F32,
        )
        later = lax.broadcasted_iota(jnp.int32, (SPAN, SPAN), 0)
        sooner = lax.broadcasted_iota(jnp.int32, (SPAN, SPAN), 1)
        scores[...] = jnp.where(later >= sooner, product, 0.0)
        half = SPAN // 2
        first = lax.broadcasted_iota(jnp.int32, (SPAN, 2 * HEAD_DIM), 1) < HEAD_DIM

        @pl.loop(0, GROUPS)
        def _(group):
            for pair in range(GROUP // 2):
                lanes = pl.ds(
                    pl.multiple_of(group * (GROUP * HEAD_DIM) + pair * 128, 128), 128
                )
                heads_in = act[rows, lanes]
                given = []
                for head in (2 * pair, 2 * pair + 1):
                    at_later = column[group, rows, head : head + 1]
                    at_sooner = row[group, head : head + 1, rows]
                    upper = scores[:half, :half] * jnp.exp2(
                        jnp.minimum(at_later[:half] - at_sooner[:, :half], 100.0)
                    )
                    lower = scores[half:, :] * jnp.exp2(
                        jnp.minimum(at_later[half:] - at_sooner, 100.0)
                    )
                    given.append(
                        jnp.concatenate(
                            [
                                jnp.dot(
                                    upper.astype(BF16), heads_in[:half],
                                    preferred_element_type=F32,
                                ),
                                jnp.dot(
                                    lower.astype(BF16), heads_in, preferred_element_type=F32
                                ),
                            ],
                            axis=0,
                        )
                    )
                total[rows, lanes] = (
                    jnp.where(first, given[0], given[1])
                    + skip[:, lanes] * heads_in.astype(F32)
                )

    @pl.when(place > 1)
    def _():
        relay()

    @pl.loop(0, INNER // CHUNK)
    def _(chunk):
        lanes = lanes_of(chunk)
        held = entering[:, lanes].astype(F32)
        for span in range(spans):
            rows = pl.ds(span * SPAN, SPAN)
            grown = jnp.dot(
                split_parts(growth[rows, :]), spread[:, lanes], preferred_element_type=F32
            )
            read = jnp.dot(
                act[rows, INNER + STATE :], held.astype(BF16), preferred_element_type=F32
            )
            out[rows, lanes] = (total[rows, lanes] + grown * read).astype(BF16)
            if span < spans - 1:
                held = decay[span : span + 1, lanes] * held + states[span, :, lanes]

    @pl.when(has_after)
    def _():
        halo_copy.wait_send()
        state_copy.wait_send()


def mixer(projected, log_decay, conv_weight, conv_bias, skip_gain):
    length = projected.shape[0]
    spans = length // SPAN
    peers = lax.axis_size("seq")
    step = -log_decay
    cum = jnp.cumsum(log_decay.reshape(HEADS, spans, SPAN), axis=2)
    last = cum[:, :, -1:]
    weight = jnp.exp(last - cum).reshape(HEADS, length) * step
    flat = cum.reshape(HEADS, length)

    def doubled(a):
        return jnp.pad(jnp.concatenate([a, a], axis=0).T, ((0, 0), (0, 128 - 2 * HEADS)))

    grouped = (flat * LOG2E).reshape(GROUPS, GROUP, length)
    column = grouped.transpose(0, 2, 1)
    row = grouped - jnp.log2(step).reshape(GROUPS, GROUP, length)
    totals = last[:, :, 0].T
    totals = jnp.concatenate([totals, jnp.sum(totals, axis=0, keepdims=True)], axis=0)
    decay = jnp.repeat(jnp.exp(totals), HEAD_DIM, axis=1)
    decay = jnp.pad(decay, ((0, -decay.shape[0] % 8), (0, 0)))
    head_of = jnp.arange(INNER)[None, :] // HEAD_DIM
    part = jnp.arange(128)[:, None]
    spread = ((part % HEADS == head_of) & (part < 2 * HEADS)).astype(BF16)
    taps = jnp.pad(conv_weight.astype(F32), ((0, 8 - CONV), (0, 0)))
    vmem = pl.BlockSpec(memory_space=pltpu.VMEM)
    return pl.pallas_call(
        functools.partial(mixer_kernel, spans, peers),
        out_shape=jax.ShapeDtypeStruct((length, INNER), BF16),
        in_specs=[vmem] * 10,
        out_specs=vmem,
        scratch_shapes=[
            pltpu.VMEM((HALO, COLS), BF16),
            pltpu.VMEM((HALO, COLS), BF16),
            pltpu.VMEM((length, COLS), BF16),
            pltpu.VMEM((STATE, SPAN), BF16),
            pltpu.VMEM((spans, STATE, INNER), F32),
            pltpu.VMEM((STATE, INNER), F32),
            pltpu.VMEM((length, INNER), F32),
            pltpu.VMEM((SPAN, SPAN), F32),
            pltpu.VMEM((STATE, INNER), BF16),
            pltpu.VMEM((STATE, INNER), BF16),
            pltpu.SemaphoreType.DMA((2,)),
            pltpu.SemaphoreType.DMA((2,)),
        ],
        compiler_params=pltpu.CompilerParams(
            collective_id=0, has_side_effects=True, vmem_limit_bytes=56 * 2**20
        ),
        cost_estimate=pl.CostEstimate(
            flops=8 * 10**9, bytes_accessed=16 * 10**6, transcendentals=12 * 10**6
        ),
        name="mixer",
    )(
        projected, taps, conv_bias[None, :], doubled(weight), doubled(jnp.exp(flat)),
        spread, decay, jnp.repeat(skip_gain, HEAD_DIM)[None, :], column, row,
    )


ORDER = (0, -1, 1, -2, 2, -3, 3)
BY_Z, BY_X, BY_Y, BY_X_HALF, BY_Y_HALF, FROM_OWN, FROM_X, FROM_Y, FROM_XY = range(9)


def gather_kernel(layers, shard, whole, send_sems, up_sems, recv_sems, own_sem):
    dp, seq = lax.axis_index("dp"), lax.axis_index("seq")
    z, x = dp // 2, lax.rem(dp, 2)
    y, core = seq // 2, lax.rem(seq, 2)
    x_peer = (z * 2 + 1 - x, seq)
    y_peer = (dp, (1 - y) * 2 + core)
    core_peer = (dp, y * 2 + 1 - core)
    above, below = (dp + 2, seq), (dp - 2, seq)
    has_above, has_below = z < layers - 1, z > 0

    barrier = pltpu.get_barrier_semaphore()

    def greet(peer):
        pl.semaphore_signal(
            barrier, inc=1, device_id=peer, device_id_type=pl.DeviceIdType.MESH
        )

    for peer in (x_peer, y_peer, core_peer):
        greet(peer)

    @pl.when(has_above)
    def _():
        greet(above)

    @pl.when(has_below)
    def _():
        greet(below)

    peers = 3 + has_above.astype(jnp.int32) + has_below.astype(jnp.int32)
    pl.semaphore_wait(barrier, peers)

    half = whole.shape[2] // 2
    low, high = pl.ds(0, half), pl.ds(half, half)

    def slot(away, other_x=False, other_y=False):
        at_x = 1 - x if other_x else x
        at_y = 1 - y if other_y else y
        return (((z + away) * 2 + at_x) * 2 + at_y) * 2 + core

    def copy(src, dst, send, recv, peer):
        return pltpu.make_async_remote_copy(
            src_ref=src, dst_ref=dst, send_sem=send, recv_sem=recv,
            device_id=peer, device_id_type=pl.DeviceIdType.MESH,
        )

    def moved(place, kind, other_x, other_y, peer, lanes=None):
        at = slot(ORDER[place], other_x, other_y)
        dst = whole.at[at] if lanes is None else whole.at[at, :, lanes]
        src = shard if place == 0 and not other_x and not other_y else dst
        return copy(src, dst, send_sems.at[place, kind], recv_sems.at[place, kind], peer)

    def by_x(place):
        return moved(place, BY_X, False, False, x_peer)

    def by_y(place):
        return moved(place, BY_Y, False, False, y_peer)

    def by_x_half(place):
        return moved(place, BY_X_HALF, False, True, x_peer, high)

    def by_y_half(place):
        return moved(place, BY_Y_HALF, True, False, y_peer, low)

    def to_core(place, kind):
        return moved(
            place, kind, kind in (FROM_X, FROM_XY), kind in (FROM_Y, FROM_XY), core_peer
        )

    def relayed(place, up):
        away = ORDER[place]
        then = ORDER.index(away - 1 if up else away + 1)
        at = slot(away)
        return copy(
            shard if place == 0 else whole.at[at], whole.at[at],
            up_sems.at[place] if up else send_sems.at[place, BY_Z],
            recv_sems.at[then, BY_Z], above if up else below,
        )

    def arrived(place, kind, other_x, other_y, lanes=None):
        at = slot(ORDER[place], other_x, other_y)
        dst = whole.at[at] if lanes is None else whole.at[at, :, lanes]
        copy(dst, dst, own_sem, recv_sems.at[place, kind], core_peer).wait_recv()

    def exists(place):
        away = ORDER[place]
        return jnp.logical_and(z + away >= 0, z + away < layers)

    def relays(place):
        away = ORDER[place]
        found = []
        if -layers + 1 < away <= 0:
            found.append((jnp.logical_and(has_above, z + away >= 0), True))
        if layers - 1 > away >= 0:
            found.append((jnp.logical_and(has_below, z + away < layers), False))
        return found

    def column_step(place):
        for there, up in relays(place):
            @pl.when(there)
            def _(up=up):
                if place and up == relays(place)[0][1]:
                    arrived(place, BY_Z, False, False)
                relayed(place, up).start()

        ends = not relays(place)

        @pl.when(exists(place))
        def _():
            if place:
                if ends:
                    arrived(place, BY_Z, False, False)
                else:
                    @pl.when(jnp.logical_not(relays(place)[0][0]))
                    def _():
                        arrived(place, BY_Z, False, False)
            by_x(place).start()
            by_y(place).start()
            to_core(place, FROM_OWN).start()

    def plane_step(place):
        @pl.when(exists(place))
        def _():
            arrived(place, BY_X, True, False)
            by_y_half(place).start()
            to_core(place, FROM_X).start()
            arrived(place, BY_Y, False, True)
            by_x_half(place).start()
            to_core(place, FROM_Y).start()

    def corner_step(place):
        @pl.when(exists(place))
        def _():
            arrived(place, BY_X_HALF, True, True, high)
            arrived(place, BY_Y_HALF, True, True, low)
            to_core(place, FROM_XY).start()

    own = pltpu.make_async_copy(shard, whole.at[slot(0)], own_sem)
    places = range(2 * layers - 1)
    for place in places:
        column_step(place)
        if place == 0:
            own.start()
        if place >= 2:
            plane_step(place - 2)
        if place >= 4:
            corner_step(place - 4)
    for place in places[-2:]:
        plane_step(place)
    for place in places[-4:]:
        corner_step(place)
    own.wait()
    for place in places:
        for there, up in relays(place):
            @pl.when(there)
            def _(up=up):
                relayed(place, up).wait_send()

        @pl.when(exists(place))
        def _():
            for sent in (
                by_x(place), by_y(place), by_x_half(place), by_y_half(place),
                to_core(place, FROM_OWN), to_core(place, FROM_X),
                to_core(place, FROM_Y), to_core(place, FROM_XY),
            ):
                sent.wait_send()
            for kind in (FROM_OWN, FROM_X, FROM_Y, FROM_XY):
                at = slot(
                    ORDER[place], kind in (FROM_X, FROM_XY), kind in (FROM_Y, FROM_XY)
                ) + 1 - 2 * core
                dst = whole.at[at]
                copy(dst, dst, own_sem, recv_sems.at[place, kind], core_peer).wait_recv()


def gathered(input_weight):
    devices = lax.axis_size("dp"), lax.axis_size("seq")
    if devices != (8, 4):
        return lax.all_gather(input_weight, ("dp", "seq"), axis=0, tiled=True)
    rows, depth = input_weight.shape
    anywhere = pl.BlockSpec(memory_space=pl.ANY)
    whole = pl.pallas_call(
        functools.partial(gather_kernel, devices[0] // 2),
        out_shape=jax.ShapeDtypeStruct((devices[0] * devices[1], rows, depth), BF16),
        in_specs=[anywhere],
        out_specs=anywhere,
        scratch_shapes=[
            pltpu.SemaphoreType.DMA((7, 9)),
            pltpu.SemaphoreType.DMA((7,)),
            pltpu.SemaphoreType.DMA((7, 9)),
            pltpu.SemaphoreType.DMA,
        ],
        compiler_params=pltpu.CompilerParams(collective_id=1, has_side_effects=True),
        name="gather",
    )(input_weight)
    return whole.reshape(devices[0] * devices[1] * rows, depth)


def body(hidden, log_decay, input_weight, conv_weight, conv_bias, skip_gain):
    projected = lax.dot_general(
        hidden[0],
        gathered(input_weight),
        NT,
        preferred_element_type=F32,
    ).astype(BF16)
    return mixer(projected, log_decay[0], conv_weight, conv_bias, skip_gain)[None]


def solution(mesh):
    placed = (P("dp", "seq", None), P("dp", None, "seq"), P(("dp", "seq"), None), P(), P(), P())
    return jax.shard_map(
        body, mesh=mesh, in_specs=placed, out_specs=P("dp", "seq", None), check_vma=False
    )
```

```python
import functools

import jax
import jax.numpy as jnp
from jax import lax
from jax.experimental import pallas as pl
from jax.experimental.pallas import tpu as pltpu
from jax.sharding import PartitionSpec as P

HEADS = 40
HEAD_DIM = 64
STATE = 128
SPAN = 256
CONV = 4
INNER = 2560
COLS = 2816
GROUP = 8
GROUPS = HEADS // GROUP
CHUNK = 256
HALO = 16
TILE = 64
LOG2E = 1.4426950408889634
F32 = jnp.float32
BF16 = jnp.bfloat16
NT = (((1,), (1,)), ((), ()))


def split_parts(both):
    high = both.astype(BF16).astype(F32)
    lane = lax.broadcasted_iota(jnp.int32, both.shape, 1)
    return jnp.where(lane < HEADS, high, both - high).astype(BF16)


def mixer_kernel(
    spans, peers,
    proj, taps, bias, weight, growth, spread, decay, skip, column, row,
    out,
    halo, previous, act, bt, states, local, total, scores, sending, entering,
    halo_sems, state_sems,
):
    place = lax.axis_index("seq")
    length = spans * SPAN
    after, before = lax.rem(place + 1, peers), lax.rem(place + peers - 1, peers)
    barrier = pltpu.get_barrier_semaphore()
    for neighbour in (before, after):
        pl.semaphore_signal(
            barrier, inc=1, device_id={"seq": neighbour}, device_id_type=pl.DeviceIdType.MESH
        )
    pl.semaphore_wait(barrier, 2)
    has_after = place < peers - 1
    has_before = place > 0

    halo_copy = pltpu.make_async_remote_copy(
        src_ref=proj.at[pl.ds(length - HALO, HALO)], dst_ref=halo,
        send_sem=halo_sems.at[0], recv_sem=halo_sems.at[1],
        device_id={"seq": after}, device_id_type=pl.DeviceIdType.MESH,
    )
    state_copy = pltpu.make_async_remote_copy(
        src_ref=sending, dst_ref=entering,
        send_sem=state_sems.at[0], recv_sem=state_sems.at[1],
        device_id={"seq": after}, device_id_type=pl.DeviceIdType.MESH,
    )

    @pl.when(has_after)
    def _():
        halo_copy.start()

    def rows_of(span):
        return pl.ds(pl.multiple_of(span * SPAN, SPAN), SPAN)

    def lanes_of(chunk, width=CHUNK):
        return pl.ds(pl.multiple_of(chunk * width, width), width)

    @pl.loop(0, spans)
    def _(lap):
        span = spans - 1 - lap
        rows = rows_of(span)

        @pl.when(span > 0)
        def _():
            start = pl.multiple_of(jnp.maximum(span * SPAN - HALO, 0), HALO)
            previous[...] = proj[pl.ds(start, HALO), :]

        @pl.when(span == 0)
        def _():
            @pl.when(has_before)
            def _():
                halo_copy.wait_recv()
                previous[...] = halo[...]

            @pl.when(jnp.logical_not(has_before))
            def _():
                previous[...] = jnp.zeros_like(previous)

        @pl.loop(0, COLS // CHUNK)
        def _(chunk):
            lanes = lanes_of(chunk)
            tap = [taps[k : k + 1, lanes] for k in range(CONV)]
            offset = bias[:, lanes]
            for part in range(SPAN // TILE):
                start = pl.multiple_of(span * SPAN + part * TILE, TILE)
                here = proj[pl.ds(start, TILE), lanes].astype(F32)
                if part == 0:
                    ahead = previous[:, lanes].astype(F32)
                else:
                    earlier = pl.multiple_of(start - HALO, HALO)
                    ahead = proj[pl.ds(earlier, HALO), lanes].astype(F32)
                both = jnp.concatenate([ahead[HALO - 8 :], here], axis=0)
                value = offset + here * tap[CONV - 1]
                for k in range(CONV - 1):
                    at = 8 - (CONV - 1) + k
                    value = value + both[at : at + TILE] * tap[k]
                act[pl.ds(start, TILE), lanes] = (value / (1.0 + jnp.exp(-value))).astype(BF16)

        bt[...] = act[rows, INNER : INNER + STATE].astype(F32).T.astype(BF16)
        parts = split_parts(weight[rows, :])

        @pl.loop(0, INNER // CHUNK)
        def _(chunk):
            lanes = lanes_of(chunk)
            scale = jnp.dot(parts, spread[:, lanes], preferred_element_type=F32)
            decayed = (act[rows, lanes].astype(F32) * scale).astype(BF16)
            states[span, :, lanes] = jnp.dot(bt[...], decayed, preferred_element_type=F32)

    @pl.loop(0, INNER // CHUNK)
    def _(chunk):
        lanes = lanes_of(chunk)
        held = states[0, :, lanes]
        for span in range(1, spans):
            held = decay[span : span + 1, lanes] * held + states[span, :, lanes]
        local[:, lanes] = held

    def relay():
        @pl.when(has_before)
        def _():
            state_copy.wait_recv()

        @pl.when(jnp.logical_not(has_before))
        def _():
            entering[...] = jnp.zeros_like(entering)

        @pl.when(has_after)
        def _():
            @pl.loop(0, INNER // CHUNK)
            def _(chunk):
                lanes = lanes_of(chunk)
                whole = decay[spans : spans + 1, lanes]
                sending[:, lanes] = (
                    whole * entering[:, lanes].astype(F32) + local[:, lanes]
                ).astype(BF16)

            state_copy.start()

    @pl.when(place <= 1)
    def _():
        relay()

    @pl.loop(0, spans)
    def _(span):
        rows = rows_of(span)
        product = lax.dot_general(
            act[rows, INNER + STATE :], act[rows, INNER : INNER + STATE], NT,
            preferred_element_type=F32,
        )
        later = lax.broadcasted_iota(jnp.int32, (SPAN, SPAN), 0)
        sooner = lax.broadcasted_iota(jnp.int32, (SPAN, SPAN), 1)
        scores[...] = jnp.where(later >= sooner, product, 0.0)
        half = SPAN // 2
        first = lax.broadcasted_iota(jnp.int32, (SPAN, 2 * HEAD_DIM), 1) < HEAD_DIM

        @pl.loop(0, GROUPS)
        def _(group):
            for pair in range(GROUP // 2):
                lanes = pl.ds(
                    pl.multiple_of(group * (GROUP * HEAD_DIM) + pair * 128, 128), 128
                )
                heads_in = act[rows, lanes]
                given = []
                for head in (2 * pair, 2 * pair + 1):
                    at_later = column[group, rows, head : head + 1]
                    at_sooner = row[group, head : head + 1, rows]
                    upper = scores[:half, :half] * jnp.exp2(
                        jnp.minimum(at_later[:half] - at_sooner[:, :half], 100.0)
                    )
                    lower = scores[half:, :] * jnp.exp2(
                        jnp.minimum(at_later[half:] - at_sooner, 100.0)
                    )
                    given.append(
                        jnp.concatenate(
                            [
                                jnp.dot(
                                    upper.astype(BF16), heads_in[:half],
                                    preferred_element_type=F32,
                                ),
                                jnp.dot(
                                    lower.astype(BF16), heads_in, preferred_element_type=F32
                                ),
                            ],
                            axis=0,
                        )
                    )
                total[rows, lanes] = (
                    jnp.where(first, given[0], given[1])
                    + skip[:, lanes] * heads_in.astype(F32)
                )

    @pl.when(place > 1)
    def _():
        relay()

    @pl.loop(0, INNER // CHUNK)
    def _(chunk):
        lanes = lanes_of(chunk)
        held = entering[:, lanes].astype(F32)
        for span in range(spans):
            rows = pl.ds(span * SPAN, SPAN)
            grown = jnp.dot(
                split_parts(growth[rows, :]), spread[:, lanes], preferred_element_type=F32
            )
            read = jnp.dot(
                act[rows, INNER + STATE :], held.astype(BF16), preferred_element_type=F32
            )
            out[rows, lanes] = (total[rows, lanes] + grown * read).astype(BF16)
            if span < spans - 1:
                held = decay[span : span + 1, lanes] * held + states[span, :, lanes]

    @pl.when(has_after)
    def _():
        halo_copy.wait_send()
        state_copy.wait_send()


def prepared(log_decay):
    length = log_decay.shape[1]
    spans = length // SPAN
    step = -log_decay
    cum = jnp.cumsum(log_decay.reshape(HEADS, spans, SPAN), axis=2)
    last = cum[:, :, -1:]
    weight = jnp.exp(last - cum).reshape(HEADS, length) * step
    flat = cum.reshape(HEADS, length)

    def doubled(a):
        return jnp.pad(jnp.concatenate([a, a], axis=0).T, ((0, 0), (0, 128 - 2 * HEADS)))

    grouped = (flat * LOG2E).reshape(GROUPS, GROUP, length)
    column = grouped.transpose(0, 2, 1)
    row = grouped - jnp.log2(step).reshape(GROUPS, GROUP, length)
    totals = last[:, :, 0].T
    totals = jnp.concatenate([totals, jnp.sum(totals, axis=0, keepdims=True)], axis=0)
    decay = jnp.repeat(jnp.exp(totals), HEAD_DIM, axis=1)
    decay = jnp.pad(decay, ((0, -decay.shape[0] % 8), (0, 0)))
    head_of = jnp.arange(INNER)[None, :] // HEAD_DIM
    part = jnp.arange(128)[:, None]
    spread = ((part % HEADS == head_of) & (part < 2 * HEADS)).astype(BF16)
    return doubled(weight), doubled(jnp.exp(flat)), spread, decay, column, row


def mixer(projected, factors, conv_weight, conv_bias, skip_gain):
    length = projected.shape[0]
    spans = length // SPAN
    peers = lax.axis_size("seq")
    weight, growth, spread, decay, column, row = factors
    taps = jnp.pad(conv_weight.astype(F32), ((0, 8 - CONV), (0, 0)))
    vmem = pl.BlockSpec(memory_space=pltpu.VMEM)
    return pl.pallas_call(
        functools.partial(mixer_kernel, spans, peers),
        out_shape=jax.ShapeDtypeStruct((length, INNER), BF16),
        in_specs=[vmem] * 10,
        out_specs=vmem,
        scratch_shapes=[
            pltpu.VMEM((HALO, COLS), BF16),
            pltpu.VMEM((HALO, COLS), BF16),
            pltpu.VMEM((length, COLS), BF16),
            pltpu.VMEM((STATE, SPAN), BF16),
            pltpu.VMEM((spans, STATE, INNER), F32),
            pltpu.VMEM((STATE, INNER), F32),
            pltpu.VMEM((length, INNER), F32),
            pltpu.VMEM((SPAN, SPAN), F32),
            pltpu.VMEM((STATE, INNER), BF16),
            pltpu.VMEM((STATE, INNER), BF16),
            pltpu.SemaphoreType.DMA((2,)),
            pltpu.SemaphoreType.DMA((2,)),
        ],
        compiler_params=pltpu.CompilerParams(
            collective_id=0, has_side_effects=True, vmem_limit_bytes=56 * 2**20
        ),
        cost_estimate=pl.CostEstimate(
            flops=8 * 10**9, bytes_accessed=16 * 10**6, transcendentals=12 * 10**6
        ),
        name="mixer",
    )(
        projected, taps, conv_bias[None, :], weight, growth, spread, decay,
        jnp.repeat(skip_gain, HEAD_DIM)[None, :], column, row,
    )


ORDER = (0, -1, 1, -2, 2, -3, 3)
BY_Z, BY_X, BY_Y, BY_X_HALF, BY_Y_HALF, FROM_OWN, FROM_X, FROM_Y, FROM_XY = range(9)


def prepare(log_decay, weight, growth, spread, decay, column, row):
    spans = log_decay.shape[1] // SPAN
    width = 2 * HEAD_DIM * 2
    for start in range(0, INNER, width):
        part = lax.broadcasted_iota(jnp.int32, (128, width), 0)
        head = jnp.where(part < HEADS, part, part - HEADS)
        gap = start + lax.broadcasted_iota(jnp.int32, (128, width), 1) - head * HEAD_DIM
        hit = (part < 2 * HEADS) & (gap >= 0) & (gap < HEAD_DIM)
        spread[:, start : start + width] = jnp.where(hit, 1.0, 0.0).astype(BF16)
    sooner = lax.broadcasted_iota(jnp.int32, (SPAN, SPAN), 0)
    later = lax.broadcasted_iota(jnp.int32, (SPAN, SPAN), 1)
    causal = jnp.where(sooner <= later, 1.0, 0.0)
    pad = jnp.zeros((128 - 2 * HEADS, SPAN), F32)
    more = jnp.zeros((128 - HEADS, SPAN), F32)
    decay[...] = jnp.ones_like(decay)
    for span in range(spans):
        rows = slice(span * SPAN, (span + 1) * SPAN)
        change = log_decay[:, rows]
        step = -change
        cum = jnp.dot(
            change, causal, precision=lax.Precision.HIGHEST, preferred_element_type=F32
        )
        left = jnp.exp(cum[:, SPAN - 1 :] - cum) * step
        grown = jnp.exp(cum)
        weight[rows, :] = jnp.concatenate([left, left, pad], axis=0).T
        growing = jnp.concatenate([grown, grown, pad], axis=0).T
        growth[rows, :] = growing
        scaled = cum * LOG2E
        turned = jnp.concatenate([scaled, more], axis=0).T
        shifted = scaled - jnp.log2(step)
        for group in range(GROUPS):
            heads = slice(group * GROUP, (group + 1) * GROUP)
            column[group, rows, :] = turned[:, heads]
            row[group, :, rows] = shifted[heads]
        ends = split_parts(growing[SPAN - 8 :, :])
        for start in range(0, INNER, width):
            lanes = slice(start, start + width)
            end = jnp.dot(ends, spread[:, lanes], preferred_element_type=F32)[7:8]
            decay[span : span + 1, lanes] = end
            decay[spans : spans + 1, lanes] = decay[spans : spans + 1, lanes] * end


def gather_kernel(
    layers, shard, log_decay,
    whole, weight, growth, spread, decay, column, row,
    send_sems, up_sems, recv_sems, own_sem,
):
    dp, seq = lax.axis_index("dp"), lax.axis_index("seq")
    z, x = dp // 2, lax.rem(dp, 2)
    y, core = seq // 2, lax.rem(seq, 2)
    x_peer = (z * 2 + 1 - x, seq)
    y_peer = (dp, (1 - y) * 2 + core)
    core_peer = (dp, y * 2 + 1 - core)
    above, below = (dp + 2, seq), (dp - 2, seq)
    has_above, has_below = z < layers - 1, z > 0

    barrier = pltpu.get_barrier_semaphore()

    def greet(peer):
        pl.semaphore_signal(
            barrier, inc=1, device_id=peer, device_id_type=pl.DeviceIdType.MESH
        )

    for peer in (x_peer, y_peer, core_peer):
        greet(peer)

    @pl.when(has_above)
    def _():
        greet(above)

    @pl.when(has_below)
    def _():
        greet(below)

    peers = 3 + has_above.astype(jnp.int32) + has_below.astype(jnp.int32)
    pl.semaphore_wait(barrier, peers)

    half = whole.shape[2] // 2
    low, high = pl.ds(0, half), pl.ds(half, half)

    def slot(away, other_x=False, other_y=False):
        at_x = 1 - x if other_x else x
        at_y = 1 - y if other_y else y
        return (((z + away) * 2 + at_x) * 2 + at_y) * 2 + core

    def copy(src, dst, send, recv, peer):
        return pltpu.make_async_remote_copy(
            src_ref=src, dst_ref=dst, send_sem=send, recv_sem=recv,
            device_id=peer, device_id_type=pl.DeviceIdType.MESH,
        )

    def moved(place, kind, other_x, other_y, peer, lanes=None):
        at = slot(ORDER[place], other_x, other_y)
        dst = whole.at[at] if lanes is None else whole.at[at, :, lanes]
        src = shard if place == 0 and not other_x and not other_y else dst
        return copy(src, dst, send_sems.at[place, kind], recv_sems.at[place, kind], peer)

    def by_x(place):
        return moved(place, BY_X, False, False, x_peer)

    def by_y(place):
        return moved(place, BY_Y, False, False, y_peer)

    def by_x_half(place):
        return moved(place, BY_X_HALF, False, True, x_peer, high)

    def by_y_half(place):
        return moved(place, BY_Y_HALF, True, False, y_peer, low)

    def to_core(place, kind):
        return moved(
            place, kind, kind in (FROM_X, FROM_XY), kind in (FROM_Y, FROM_XY), core_peer
        )

    def relayed(place, up):
        away = ORDER[place]
        then = ORDER.index(away - 1 if up else away + 1)
        at = slot(away)
        return copy(
            shard if place == 0 else whole.at[at], whole.at[at],
            up_sems.at[place] if up else send_sems.at[place, BY_Z],
            recv_sems.at[then, BY_Z], above if up else below,
        )

    def arrived(place, kind, other_x, other_y, lanes=None):
        at = slot(ORDER[place], other_x, other_y)
        dst = whole.at[at] if lanes is None else whole.at[at, :, lanes]
        copy(dst, dst, own_sem, recv_sems.at[place, kind], core_peer).wait_recv()

    def exists(place):
        away = ORDER[place]
        return jnp.logical_and(z + away >= 0, z + away < layers)

    def relays(place):
        away = ORDER[place]
        found = []
        if -layers + 1 < away <= 0:
            found.append((jnp.logical_and(has_above, z + away >= 0), True))
        if layers - 1 > away >= 0:
            found.append((jnp.logical_and(has_below, z + away < layers), False))
        return found

    def column_step(place):
        for there, up in relays(place):
            @pl.when(there)
            def _(up=up):
                if place and up == relays(place)[0][1]:
                    arrived(place, BY_Z, False, False)
                relayed(place, up).start()

        ends = not relays(place)

        @pl.when(exists(place))
        def _():
            if place:
                if ends:
                    arrived(place, BY_Z, False, False)
                else:
                    @pl.when(jnp.logical_not(relays(place)[0][0]))
                    def _():
                        arrived(place, BY_Z, False, False)
            by_x(place).start()
            by_y(place).start()
            to_core(place, FROM_OWN).start()

    def plane_step(place):
        @pl.when(exists(place))
        def _():
            arrived(place, BY_X, True, False)
            by_y_half(place).start()
            to_core(place, FROM_X).start()
            arrived(place, BY_Y, False, True)
            by_x_half(place).start()
            to_core(place, FROM_Y).start()

    def corner_step(place):
        @pl.when(exists(place))
        def _():
            arrived(place, BY_X_HALF, True, True, high)
            arrived(place, BY_Y_HALF, True, True, low)
            to_core(place, FROM_XY).start()

    own = pltpu.make_async_copy(shard, whole.at[slot(0)], own_sem)
    places = range(2 * layers - 1)
    for place in places:
        column_step(place)
        if place == 0:
            own.start()
            prepare(log_decay, weight, growth, spread, decay, column, row)
        if place >= 2:
            plane_step(place - 2)
        if place >= 4:
            corner_step(place - 4)
    for place in places[-2:]:
        plane_step(place)
    for place in places[-4:]:
        corner_step(place)
    own.wait()
    for place in places:
        for there, up in relays(place):
            @pl.when(there)
            def _(up=up):
                relayed(place, up).wait_send()

        @pl.when(exists(place))
        def _():
            for sent in (
                by_x(place), by_y(place), by_x_half(place), by_y_half(place),
                to_core(place, FROM_OWN), to_core(place, FROM_X),
                to_core(place, FROM_Y), to_core(place, FROM_XY),
            ):
                sent.wait_send()
            for kind in (FROM_OWN, FROM_X, FROM_Y, FROM_XY):
                at = slot(
                    ORDER[place], kind in (FROM_X, FROM_XY), kind in (FROM_Y, FROM_XY)
                ) + 1 - 2 * core
                dst = whole.at[at]
                copy(dst, dst, own_sem, recv_sems.at[place, kind], core_peer).wait_recv()


def gathered(input_weight, log_decay):
    devices = lax.axis_size("dp"), lax.axis_size("seq")
    rows, depth = input_weight.shape
    length = log_decay.shape[1]
    if devices != (8, 4) or length // SPAN > 7:
        whole = lax.all_gather(input_weight, ("dp", "seq"), axis=0, tiled=True)
        return whole, prepared(log_decay)
    anywhere = pl.BlockSpec(memory_space=pl.ANY)
    vmem = pl.BlockSpec(memory_space=pltpu.VMEM)
    whole, *factors = pl.pallas_call(
        functools.partial(gather_kernel, devices[0] // 2),
        out_shape=[
            jax.ShapeDtypeStruct((devices[0] * devices[1], rows, depth), BF16),
            jax.ShapeDtypeStruct((length, 128), F32),
            jax.ShapeDtypeStruct((length, 128), F32),
            jax.ShapeDtypeStruct((128, INNER), BF16),
            jax.ShapeDtypeStruct((8, INNER), F32),
            jax.ShapeDtypeStruct((GROUPS, length, GROUP), F32),
            jax.ShapeDtypeStruct((GROUPS, GROUP, length), F32),
        ],
        in_specs=[anywhere, vmem],
        out_specs=[anywhere] + [vmem] * 6,
        scratch_shapes=[
            pltpu.SemaphoreType.DMA((7, 9)),
            pltpu.SemaphoreType.DMA((7,)),
            pltpu.SemaphoreType.DMA((7, 9)),
            pltpu.SemaphoreType.DMA,
        ],
        compiler_params=pltpu.CompilerParams(
            collective_id=1, has_side_effects=True, vmem_limit_bytes=20 * 2**20
        ),
        name="gather",
    )(input_weight, log_decay)
    return whole.reshape(devices[0] * devices[1] * rows, depth), factors


def body(hidden, log_decay, input_weight, conv_weight, conv_bias, skip_gain):
    whole, factors = gathered(input_weight, log_decay[0])
    projected = lax.dot_general(
        hidden[0], whole, NT, preferred_element_type=F32
    ).astype(BF16)
    return mixer(projected, factors, conv_weight, conv_bias, skip_gain)[None]


def solution(mesh):
    placed = (P("dp", "seq", None), P("dp", None, "seq"), P(("dp", "seq"), None), P(), P(), P())
    return jax.shard_map(
        body, mesh=mesh, in_specs=placed, out_specs=P("dp", "seq", None), check_vma=False
    )
```

```python
import functools

import jax
import jax.numpy as jnp
from jax import lax
from jax.experimental import pallas as pl
from jax.experimental.pallas import tpu as pltpu
from jax.sharding import PartitionSpec as P

HEADS = 40
HEAD_DIM = 64
STATE = 128
SPAN = 256
CONV = 4
INNER = 2560
COLS = 2816
GROUP = 8
GROUPS = HEADS // GROUP
CHUNK = 256
HALO = 16
TILE = 64
LOG2E = 1.4426950408889634
F32 = jnp.float32
BF16 = jnp.bfloat16
NT = (((1,), (1,)), ((), ()))


def split_parts(both):
    high = both.astype(BF16).astype(F32)
    lane = lax.broadcasted_iota(jnp.int32, both.shape, 1)
    return jnp.where(lane < HEADS, high, both - high).astype(BF16)


def mixer_kernel(
    spans, peers,
    proj, taps, bias, weight, growth, spread, decay, skip, column, row,
    out,
    halo, previous, act, bt, states, local, total, scores, sending, entering, growing,
    halo_sems, state_sems,
):
    place = lax.axis_index("seq")
    length = spans * SPAN
    after, before = lax.rem(place + 1, peers), lax.rem(place + peers - 1, peers)
    barrier = pltpu.get_barrier_semaphore()
    for neighbour in (before, after):
        pl.semaphore_signal(
            barrier, inc=1, device_id={"seq": neighbour}, device_id_type=pl.DeviceIdType.MESH
        )
    pl.semaphore_wait(barrier, 2)
    has_after = place < peers - 1
    has_before = place > 0

    halo_copy = pltpu.make_async_remote_copy(
        src_ref=proj.at[pl.ds(length - HALO, HALO)], dst_ref=halo,
        send_sem=halo_sems.at[0], recv_sem=halo_sems.at[1],
        device_id={"seq": after}, device_id_type=pl.DeviceIdType.MESH,
    )
    state_copy = pltpu.make_async_remote_copy(
        src_ref=sending, dst_ref=entering,
        send_sem=state_sems.at[0], recv_sem=state_sems.at[1],
        device_id={"seq": after}, device_id_type=pl.DeviceIdType.MESH,
    )

    @pl.when(has_after)
    def _():
        halo_copy.start()

    def rows_of(span):
        return pl.ds(pl.multiple_of(span * SPAN, SPAN), SPAN)

    def lanes_of(chunk, width=CHUNK):
        return pl.ds(pl.multiple_of(chunk * width, width), width)

    @pl.loop(0, spans)
    def _(lap):
        span = spans - 1 - lap
        rows = rows_of(span)

        @pl.when(span > 0)
        def _():
            start = pl.multiple_of(jnp.maximum(span * SPAN - HALO, 0), HALO)
            previous[...] = proj[pl.ds(start, HALO), :]

        @pl.when(span == 0)
        def _():
            @pl.when(has_before)
            def _():
                halo_copy.wait_recv()
                previous[...] = halo[...]

            @pl.when(jnp.logical_not(has_before))
            def _():
                previous[...] = jnp.zeros_like(previous)

        @pl.loop(0, COLS // CHUNK)
        def _(chunk):
            lanes = lanes_of(chunk)
            tap = [taps[k : k + 1, lanes] for k in range(CONV)]
            offset = bias[:, lanes]
            for part in range(SPAN // TILE):
                start = pl.multiple_of(span * SPAN + part * TILE, TILE)
                here = proj[pl.ds(start, TILE), lanes].astype(F32)
                if part == 0:
                    ahead = previous[:, lanes].astype(F32)
                else:
                    earlier = pl.multiple_of(start - HALO, HALO)
                    ahead = proj[pl.ds(earlier, HALO), lanes].astype(F32)
                both = jnp.concatenate([ahead[HALO - 8 :], here], axis=0)
                value = offset + here * tap[CONV - 1]
                for k in range(CONV - 1):
                    at = 8 - (CONV - 1) + k
                    value = value + both[at : at + TILE] * tap[k]
                halved = 0.5 * value
                act[pl.ds(start, TILE), lanes] = (halved + halved * jnp.tanh(halved)).astype(BF16)

        bt[...] = act[rows, INNER : INNER + STATE].astype(F32).T.astype(BF16)
        parts = split_parts(weight[rows, :])
        growing[rows, :] = split_parts(growth[rows, :])

        @pl.loop(0, INNER // CHUNK)
        def _(chunk):
            lanes = lanes_of(chunk)
            scale = jnp.dot(parts, spread[:, lanes], preferred_element_type=F32)
            decayed = (act[rows, lanes].astype(F32) * scale).astype(BF16)
            states[span, :, lanes] = jnp.dot(bt[...], decayed, preferred_element_type=F32)

    @pl.loop(0, INNER // CHUNK)
    def _(chunk):
        lanes = lanes_of(chunk)
        held = states[0, :, lanes]
        for span in range(1, spans):
            held = decay[span : span + 1, lanes] * held + states[span, :, lanes]
        local[:, lanes] = held

    def relay():
        @pl.when(has_before)
        def _():
            state_copy.wait_recv()

        @pl.when(jnp.logical_not(has_before))
        def _():
            entering[...] = jnp.zeros_like(entering)

        @pl.when(has_after)
        def _():
            @pl.loop(0, INNER // CHUNK)
            def _(chunk):
                lanes = lanes_of(chunk)
                whole = decay[spans : spans + 1, lanes]
                sending[:, lanes] = (
                    whole * entering[:, lanes].astype(F32) + local[:, lanes]
                ).astype(BF16)

            state_copy.start()

    @pl.when(place <= 1)
    def _():
        relay()

    @pl.loop(0, spans)
    def _(span):
        rows = rows_of(span)
        product = lax.dot_general(
            act[rows, INNER + STATE :], act[rows, INNER : INNER + STATE], NT,
            preferred_element_type=F32,
        )
        later = lax.broadcasted_iota(jnp.int32, (SPAN, SPAN), 0)
        sooner = lax.broadcasted_iota(jnp.int32, (SPAN, SPAN), 1)
        scores[...] = jnp.where(later >= sooner, product, 0.0)
        half = SPAN // 2
        first = lax.broadcasted_iota(jnp.int32, (SPAN, 2 * HEAD_DIM), 1) < HEAD_DIM

        @pl.loop(0, GROUPS)
        def _(group):
            for pair in range(GROUP // 2):
                lanes = pl.ds(
                    pl.multiple_of(group * (GROUP * HEAD_DIM) + pair * 128, 128), 128
                )
                heads_in = act[rows, lanes]
                given = []
                for head in (2 * pair, 2 * pair + 1):
                    at_later = column[group, rows, head : head + 1]
                    at_sooner = row[group, head : head + 1, rows]
                    upper = scores[:half, :half] * jnp.exp2(
                        jnp.minimum(at_later[:half] - at_sooner[:, :half], 100.0)
                    )
                    lower = scores[half:, :] * jnp.exp2(
                        jnp.minimum(at_later[half:] - at_sooner, 100.0)
                    )
                    given.append(
                        jnp.concatenate(
                            [
                                jnp.dot(
                                    upper.astype(BF16), heads_in[:half],
                                    preferred_element_type=F32,
                                ),
                                jnp.dot(
                                    lower.astype(BF16), heads_in, preferred_element_type=F32
                                ),
                            ],
                            axis=0,
                        )
                    )
                total[rows, lanes] = (
                    jnp.where(first, given[0], given[1])
                    + skip[:, lanes] * heads_in.astype(F32)
                )

    @pl.when(place > 1)
    def _():
        relay()

    @pl.loop(0, INNER // CHUNK)
    def _(chunk):
        lanes = lanes_of(chunk)
        held = entering[:, lanes].astype(F32)
        for span in range(spans):
            rows = pl.ds(span * SPAN, SPAN)
            grown = jnp.dot(growing[rows, :], spread[:, lanes], preferred_element_type=F32)
            read = jnp.dot(
                act[rows, INNER + STATE :], held.astype(BF16), preferred_element_type=F32
            )
            out[rows, lanes] = (total[rows, lanes] + grown * read).astype(BF16)
            if span < spans - 1:
                held = decay[span : span + 1, lanes] * held + states[span, :, lanes]

    @pl.when(has_after)
    def _():
        halo_copy.wait_send()
        state_copy.wait_send()


def prepared(log_decay):
    length = log_decay.shape[1]
    spans = length // SPAN
    step = -log_decay
    cum = jnp.cumsum(log_decay.reshape(HEADS, spans, SPAN), axis=2)
    last = cum[:, :, -1:]
    weight = jnp.exp(last - cum).reshape(HEADS, length) * step
    flat = cum.reshape(HEADS, length)

    def doubled(a):
        return jnp.pad(jnp.concatenate([a, a], axis=0).T, ((0, 0), (0, 128 - 2 * HEADS)))

    grouped = (flat * LOG2E).reshape(GROUPS, GROUP, length)
    column = grouped.transpose(0, 2, 1)
    row = grouped - jnp.log2(step).reshape(GROUPS, GROUP, length)
    totals = last[:, :, 0].T
    totals = jnp.concatenate([totals, jnp.sum(totals, axis=0, keepdims=True)], axis=0)
    decay = jnp.repeat(jnp.exp(totals), HEAD_DIM, axis=1)
    decay = jnp.pad(decay, ((0, -decay.shape[0] % 8), (0, 0)))
    head_of = jnp.arange(INNER)[None, :] // HEAD_DIM
    part = jnp.arange(128)[:, None]
    spread = ((part % HEADS == head_of) & (part < 2 * HEADS)).astype(BF16)
    return doubled(weight), doubled(jnp.exp(flat)), spread, decay, column, row


def mixer(projected, factors, conv_weight, conv_bias, skip_gain):
    length = projected.shape[0]
    spans = length // SPAN
    peers = lax.axis_size("seq")
    weight, growth, spread, decay, column, row = factors
    taps = jnp.pad(conv_weight.astype(F32), ((0, 8 - CONV), (0, 0)))
    vmem = pl.BlockSpec(memory_space=pltpu.VMEM)
    return pl.pallas_call(
        functools.partial(mixer_kernel, spans, peers),
        out_shape=jax.ShapeDtypeStruct((length, INNER), BF16),
        in_specs=[vmem] * 10,
        out_specs=vmem,
        scratch_shapes=[
            pltpu.VMEM((HALO, COLS), BF16),
            pltpu.VMEM((HALO, COLS), BF16),
            pltpu.VMEM((length, COLS), BF16),
            pltpu.VMEM((STATE, SPAN), BF16),
            pltpu.VMEM((spans, STATE, INNER), F32),
            pltpu.VMEM((STATE, INNER), F32),
            pltpu.VMEM((length, INNER), F32),
            pltpu.VMEM((SPAN, SPAN), F32),
            pltpu.VMEM((STATE, INNER), BF16),
            pltpu.VMEM((STATE, INNER), BF16),
            pltpu.VMEM((length, 128), BF16),
            pltpu.SemaphoreType.DMA((2,)),
            pltpu.SemaphoreType.DMA((2,)),
        ],
        compiler_params=pltpu.CompilerParams(
            collective_id=0, has_side_effects=True, vmem_limit_bytes=56 * 2**20
        ),
        cost_estimate=pl.CostEstimate(
            flops=8 * 10**9, bytes_accessed=16 * 10**6, transcendentals=12 * 10**6
        ),
        name="mixer",
    )(
        projected, taps, conv_bias[None, :], weight, growth, spread, decay,
        jnp.repeat(skip_gain, HEAD_DIM)[None, :], column, row,
    )


ORDER = (0, -1, 1, -2, 2, -3, 3)
BY_Z, BY_X, BY_Y, BY_X_HALF, BY_Y_HALF, FROM_OWN, FROM_X, FROM_Y, FROM_XY = range(9)


def prepare(log_decay, weight, growth, spread, decay, column, row):
    spans = log_decay.shape[1] // SPAN
    width = 2 * HEAD_DIM * 2
    for start in range(0, INNER, width):
        part = lax.broadcasted_iota(jnp.int32, (128, width), 0)
        head = jnp.where(part < HEADS, part, part - HEADS)
        gap = start + lax.broadcasted_iota(jnp.int32, (128, width), 1) - head * HEAD_DIM
        hit = (part < 2 * HEADS) & (gap >= 0) & (gap < HEAD_DIM)
        spread[:, start : start + width] = jnp.where(hit, 1.0, 0.0).astype(BF16)
    sooner = lax.broadcasted_iota(jnp.int32, (SPAN, SPAN), 0)
    later = lax.broadcasted_iota(jnp.int32, (SPAN, SPAN), 1)
    causal = jnp.where(sooner <= later, 1.0, 0.0)
    pad = jnp.zeros((128 - 2 * HEADS, SPAN), F32)
    more = jnp.zeros((128 - HEADS, SPAN), F32)
    decay[...] = jnp.ones_like(decay)
    for span in range(spans):
        rows = slice(span * SPAN, (span + 1) * SPAN)
        change = log_decay[:, rows]
        step = -change
        cum = jnp.dot(
            change, causal, precision=lax.Precision.HIGHEST, preferred_element_type=F32
        )
        left = jnp.exp(cum[:, SPAN - 1 :] - cum) * step
        grown = jnp.exp(cum)
        weight[rows, :] = jnp.concatenate([left, left, pad], axis=0).T
        growing = jnp.concatenate([grown, grown, pad], axis=0).T
        growth[rows, :] = growing
        scaled = cum * LOG2E
        turned = jnp.concatenate([scaled, more], axis=0).T
        shifted = scaled - jnp.log2(step)
        for group in range(GROUPS):
            heads = slice(group * GROUP, (group + 1) * GROUP)
            column[group, rows, :] = turned[:, heads]
            row[group, :, rows] = shifted[heads]
        ends = split_parts(growing[SPAN - 8 :, :])
        for start in range(0, INNER, width):
            lanes = slice(start, start + width)
            end = jnp.dot(ends, spread[:, lanes], preferred_element_type=F32)[7:8]
            decay[span : span + 1, lanes] = end
            decay[spans : spans + 1, lanes] = decay[spans : spans + 1, lanes] * end


def gather_kernel(
    layers, shard, log_decay,
    whole, weight, growth, spread, decay, column, row,
    send_sems, up_sems, recv_sems, own_sem,
):
    dp, seq = lax.axis_index("dp"), lax.axis_index("seq")
    z, x = dp // 2, lax.rem(dp, 2)
    y, core = seq // 2, lax.rem(seq, 2)
    x_peer = (z * 2 + 1 - x, seq)
    y_peer = (dp, (1 - y) * 2 + core)
    core_peer = (dp, y * 2 + 1 - core)
    above, below = (dp + 2, seq), (dp - 2, seq)
    has_above, has_below = z < layers - 1, z > 0

    barrier = pltpu.get_barrier_semaphore()

    def greet(peer):
        pl.semaphore_signal(
            barrier, inc=1, device_id=peer, device_id_type=pl.DeviceIdType.MESH
        )

    for peer in (x_peer, y_peer, core_peer):
        greet(peer)

    @pl.when(has_above)
    def _():
        greet(above)

    @pl.when(has_below)
    def _():
        greet(below)

    peers = 3 + has_above.astype(jnp.int32) + has_below.astype(jnp.int32)
    pl.semaphore_wait(barrier, peers)

    half = whole.shape[2] // 2
    low, high = pl.ds(0, half), pl.ds(half, half)

    def slot(away, other_x=False, other_y=False):
        at_x = 1 - x if other_x else x
        at_y = 1 - y if other_y else y
        return (((z + away) * 2 + at_x) * 2 + at_y) * 2 + core

    def copy(src, dst, send, recv, peer):
        return pltpu.make_async_remote_copy(
            src_ref=src, dst_ref=dst, send_sem=send, recv_sem=recv,
            device_id=peer, device_id_type=pl.DeviceIdType.MESH,
        )

    def moved(place, kind, other_x, other_y, peer, lanes=None):
        at = slot(ORDER[place], other_x, other_y)
        dst = whole.at[at] if lanes is None else whole.at[at, :, lanes]
        src = shard if place == 0 and not other_x and not other_y else dst
        return copy(src, dst, send_sems.at[place, kind], recv_sems.at[place, kind], peer)

    def by_x(place):
        return moved(place, BY_X, False, False, x_peer)

    def by_y(place):
        return moved(place, BY_Y, False, False, y_peer)

    def by_x_half(place):
        return moved(place, BY_X_HALF, False, True, x_peer, high)

    def by_y_half(place):
        return moved(place, BY_Y_HALF, True, False, y_peer, low)

    def to_core(place, kind):
        return moved(
            place, kind, kind in (FROM_X, FROM_XY), kind in (FROM_Y, FROM_XY), core_peer
        )

    def relayed(place, up):
        away = ORDER[place]
        then = ORDER.index(away - 1 if up else away + 1)
        at = slot(away)
        return copy(
            shard if place == 0 else whole.at[at], whole.at[at],
            up_sems.at[place] if up else send_sems.at[place, BY_Z],
            recv_sems.at[then, BY_Z], above if up else below,
        )

    def arrived(place, kind, other_x, other_y, lanes=None):
        at = slot(ORDER[place], other_x, other_y)
        dst = whole.at[at] if lanes is None else whole.at[at, :, lanes]
        copy(dst, dst, own_sem, recv_sems.at[place, kind], core_peer).wait_recv()

    def exists(place):
        away = ORDER[place]
        return jnp.logical_and(z + away >= 0, z + away < layers)

    def relays(place):
        away = ORDER[place]
        found = []
        if -layers + 1 < away <= 0:
            found.append((jnp.logical_and(has_above, z + away >= 0), True))
        if layers - 1 > away >= 0:
            found.append((jnp.logical_and(has_below, z + away < layers), False))
        return found

    def column_step(place):
        for there, up in relays(place):
            @pl.when(there)
            def _(up=up):
                if place and up == relays(place)[0][1]:
                    arrived(place, BY_Z, False, False)
                relayed(place, up).start()

        ends = not relays(place)

        @pl.when(exists(place))
        def _():
            if place:
                if ends:
                    arrived(place, BY_Z, False, False)
                else:
                    @pl.when(jnp.logical_not(relays(place)[0][0]))
                    def _():
                        arrived(place, BY_Z, False, False)
            by_x(place).start()
            by_y(place).start()
            to_core(place, FROM_OWN).start()

    def plane_step(place):
        @pl.when(exists(place))
        def _():
            arrived(place, BY_X, True, False)
            by_y_half(place).start()
            to_core(place, FROM_X).start()
            arrived(place, BY_Y, False, True)
            by_x_half(place).start()
            to_core(place, FROM_Y).start()

    def corner_step(place):
        @pl.when(exists(place))
        def _():
            arrived(place, BY_X_HALF, True, True, high)
            arrived(place, BY_Y_HALF, True, True, low)
            to_core(place, FROM_XY).start()

    own = pltpu.make_async_copy(shard, whole.at[slot(0)], own_sem)
    places = range(2 * layers - 1)
    for place in places:
        column_step(place)
        if place == 0:
            own.start()
            prepare(log_decay, weight, growth, spread, decay, column, row)
        if place >= 2:
            plane_step(place - 2)
        if place >= 4:
            corner_step(place - 4)
    for place in places[-2:]:
        plane_step(place)
    for place in places[-4:]:
        corner_step(place)
    own.wait()
    for place in places:
        for there, up in relays(place):
            @pl.when(there)
            def _(up=up):
                relayed(place, up).wait_send()

        @pl.when(exists(place))
        def _():
            for sent in (
                by_x(place), by_y(place), by_x_half(place), by_y_half(place),
                to_core(place, FROM_OWN), to_core(place, FROM_X),
                to_core(place, FROM_Y), to_core(place, FROM_XY),
            ):
                sent.wait_send()
            for kind in (FROM_OWN, FROM_X, FROM_Y, FROM_XY):
                at = slot(
                    ORDER[place], kind in (FROM_X, FROM_XY), kind in (FROM_Y, FROM_XY)
                ) + 1 - 2 * core
                dst = whole.at[at]
                copy(dst, dst, own_sem, recv_sems.at[place, kind], core_peer).wait_recv()


def gathered(input_weight, log_decay):
    devices = lax.axis_size("dp"), lax.axis_size("seq")
    rows, depth = input_weight.shape
    length = log_decay.shape[1]
    if devices != (8, 4) or length // SPAN > 7:
        whole = lax.all_gather(input_weight, ("dp", "seq"), axis=0, tiled=True)
        return whole, prepared(log_decay)
    anywhere = pl.BlockSpec(memory_space=pl.ANY)
    vmem = pl.BlockSpec(memory_space=pltpu.VMEM)
    whole, *factors = pl.pallas_call(
        functools.partial(gather_kernel, devices[0] // 2),
        out_shape=[
            jax.ShapeDtypeStruct((devices[0] * devices[1], rows, depth), BF16),
            jax.ShapeDtypeStruct((length, 128), F32),
            jax.ShapeDtypeStruct((length, 128), F32),
            jax.ShapeDtypeStruct((128, INNER), BF16),
            jax.ShapeDtypeStruct((8, INNER), F32),
            jax.ShapeDtypeStruct((GROUPS, length, GROUP), F32),
            jax.ShapeDtypeStruct((GROUPS, GROUP, length), F32),
        ],
        in_specs=[anywhere, vmem],
        out_specs=[anywhere] + [vmem] * 6,
        scratch_shapes=[
            pltpu.SemaphoreType.DMA((7, 9)),
            pltpu.SemaphoreType.DMA((7,)),
            pltpu.SemaphoreType.DMA((7, 9)),
            pltpu.SemaphoreType.DMA,
        ],
        compiler_params=pltpu.CompilerParams(
            collective_id=1, has_side_effects=True, vmem_limit_bytes=20 * 2**20
        ),
        name="gather",
    )(input_weight, log_decay)
    return whole.reshape(devices[0] * devices[1] * rows, depth), factors


def body(hidden, log_decay, input_weight, conv_weight, conv_bias, skip_gain):
    whole, factors = gathered(input_weight, log_decay[0])
    projected = lax.dot_general(
        hidden[0], whole, NT, preferred_element_type=F32
    ).astype(BF16)
    return mixer(projected, factors, conv_weight, conv_bias, skip_gain)[None]


def solution(mesh):
    placed = (P("dp", "seq", None), P("dp", None, "seq"), P(("dp", "seq"), None), P(), P(), P())
    return jax.shard_map(
        body, mesh=mesh, in_specs=placed, out_specs=P("dp", "seq", None), check_vma=False
    )
```
